32 devices in a mesh: groups: 2 (over x), fsdp: 16 (over z, y, core).
Axes of the slice: x: 2, y: 2, z: 4, core: 2. Of those that a mesh axis runs over, the one named last changes fastest.
Arguments:
- inputs: bfloat16 [4096, 4096], P(('groups', 'fsdp')), parts along dimension 0, may hold values from -6 to 6
- cotangent: bfloat16 [4096, 4096], P(('groups', 'fsdp')), parts along dimension 0, may hold values from -6 to 6
- tile_store: bfloat16 [256, 128, 128], P('fsdp'), may hold values from -0.5 to 0.5
- pattern: int32 [2, 40], replicated, may hold values from 0 to 111, as said below
- tile_slot: int32 [3, 40], replicated, may hold values from 0 to 255, as said below
Outputs:
- output: bfloat16 [4096, 4096], P(('groups', 'fsdp')), parts along dimension 0
- input_grad: bfloat16 [4096, 4096], P(('groups', 'fsdp')), parts along dimension 0
- tile_grads: float32 [512, 128, 128], P(('groups', 'fsdp')), parts along dimension 0
The draws below stay inside these ranges and needn't reach their ends.
There are 2 independent parts, one for each index of `groups`. The reference program is written for one: setup_inputs(seed, part) draws one part's arguments, and reference() takes and returns one part's arrays. A program takes and returns all parts, laid end to end along the dimension named above; an argument that names none is the same for every part. Nothing has to cross between parts.
Inputs may be any that keep to these rules, and one draw needn't show every extreme that they name: The 40 pairs (pattern[0, j], pattern[1, j]) are distinct; pattern[0] lies below 32, pattern[1] below 112. `tile_slot`: all 120 entries are distinct. Slot s belongs to device s // 16 of fsdp; at least one device holds tiles in all of its 16 slots.
All inputs are finite; a program needn't handle non-finite values.
Results may differ from the reference program's by a relative error of at most 0.0049.
Values may be sent and summed in bfloat16 or wider, within the bound.
A program may use at most 128 MiB of HBM per device.

```python
import jax
import jax.numpy as jnp
from jax import lax

D = 4096
FF = 14336
TILE = 128
TILES = 40
TOK_DEV = 128
TOKENS = 2048
CAP = 16
N_FSDP = 16


def draw_pattern(key, part):
    key = jax.random.fold_in(key, 11)
    col_blocks = FF // TILE
    cells = jax.random.permutation(key, D // TILE * col_blocks)[:TILES]
    return jnp.stack([cells // col_blocks, cells % col_blocks]).astype(jnp.int32)


def draw_tile_slot(key, part):
    key = jax.random.fold_in(key, 23)
    first_key, second_key, third_key = jax.random.split(key, 3)
    total = N_FSDP * CAP
    busiest = jax.random.randint(first_key, (), 0, N_FSDP).astype(jnp.int32)
    others = jax.random.permutation(second_key, total - CAP).astype(jnp.int32)
    placed = (busiest * CAP + CAP + others) % total
    filled = busiest * CAP + jnp.arange(CAP, dtype=jnp.int32)
    slots = jnp.concatenate([filled, placed[:3 * TILES - CAP]])
    order = jax.random.permutation(third_key, 3 * TILES)
    return slots[order].reshape(3, TILES).astype(jnp.int32)


def level_of(key, extent, cuts, smallest, largest):
    def one(dim, blocks):
        draws = jax.random.uniform(jax.random.fold_in(jax.random.fold_in(key, 6), dim), (blocks,), jnp.float32, smallest / len(cuts), largest / len(cuts))
        return jnp.repeat(jnp.exp(draws), extent[dim] // blocks).reshape((-1,) + (1,) * (len(extent) - dim - 1))

    factor_of = one(*cuts[0])
    for cut in cuts[1:]:
        factor_of = factor_of * one(*cut)
    return factor_of


def normal_values(key, dims, spread, reach, cuts=(), held_as=jnp.bfloat16):
    array = jax.random.normal(key, dims, jnp.float32) * spread
    if len(cuts) > 0:
        array = level_of(key, dims, cuts, -0.22, 0.18) * array
    return jnp.clip(array, min=-reach, max=reach).astype(held_as)


def setup_inputs(seed: int = 0, part: int = 0) -> dict:
    keys = jax.random.split(jax.random.key(seed), 6)
    own_keys = jax.random.split(jax.random.fold_in(keys[5], part), 6)
    return {
        "inputs": normal_values(own_keys[0], (TOKENS, D), 1.0, 6.0, ((0, 16),)),
        "cotangent": normal_values(own_keys[1], (TOKENS, D), 1.0, 6.0, ((0, 16),)),
        "tile_store": normal_values(keys[2], (N_FSDP * CAP, TILE, TILE), TILE ** -0.5, 0.5, ((0, 16),)),
        "pattern": draw_pattern(jax.random.fold_in(keys[5], 71), part),
        "tile_slot": draw_tile_slot(jax.random.fold_in(keys[5], 71), part),
    }


def block_pass(tok_rows, cot_rows, w_gate, w_up, w_down, row_index, col_index):
    n_rows = tok_rows.shape[0]
    row_blocks = D // TILE
    col_blocks = FF // TILE
    tok_tiles = jnp.take(tok_rows.reshape(n_rows, row_blocks, TILE), row_index, axis=1).astype(jnp.float32)
    cot_tiles = jnp.take(cot_rows.reshape(n_rows, row_blocks, TILE), row_index, axis=1).astype(jnp.float32)
    gate_w = w_gate.astype(jnp.float32)
    up_w = w_up.astype(jnp.float32)
    down_w = w_down.astype(jnp.float32)
    gate = jax.ops.segment_sum(jnp.einsum("tjd,jdf->jtf", tok_tiles, gate_w), col_index, num_segments=col_blocks)
    up = jax.ops.segment_sum(jnp.einsum("tjd,jdf->jtf", tok_tiles, up_w), col_index, num_segments=col_blocks)
    sigmoid_gate = jax.nn.sigmoid(gate)
    activated = gate * sigmoid_gate
    hidden = (activated * up).astype(jnp.bfloat16)
    hidden_tiles = hidden[col_index].astype(jnp.float32)
    output = jax.ops.segment_sum(jnp.einsum("jtf,jfd->jtd", hidden_tiles, down_w), row_index, num_segments=row_blocks)
    output = output.transpose(1, 0, 2).reshape(n_rows, D).astype(jnp.bfloat16)
    d_hidden = jax.ops.segment_sum(jnp.einsum("tjd,jfd->jtf", cot_tiles, down_w), col_index, num_segments=col_blocks)
    d_gate = (d_hidden * up * sigmoid_gate * (1.0 + gate * (1.0 - sigmoid_gate))).astype(jnp.bfloat16)
    d_up = (d_hidden * activated).astype(jnp.bfloat16)
    gate_tiles = d_gate[col_index].astype(jnp.float32)
    up_tiles = d_up[col_index].astype(jnp.float32)
    back = jnp.einsum("jtf,jdf->jtd", gate_tiles, gate_w) + jnp.einsum("jtf,jdf->jtd", up_tiles, up_w)
    input_grad = jax.ops.segment_sum(back, row_index, num_segments=row_blocks)
    input_grad = input_grad.transpose(1, 0, 2).reshape(n_rows, D).astype(jnp.bfloat16)
    grad_gate = jnp.einsum("tjd,jtf->jdf", tok_tiles, gate_tiles)
    grad_up = jnp.einsum("tjd,jtf->jdf", tok_tiles, up_tiles)
    grad_down = jnp.einsum("jtf,tjd->jfd", hidden_tiles, cot_tiles)
    return output, input_grad, jnp.stack([grad_gate, grad_up, grad_down])


def reference(inputs, cotangent, tile_store, pattern, tile_slot):
    row_index = pattern[0]
    col_index = pattern[1]
    w_gate = tile_store[tile_slot[0]]
    w_up = tile_store[tile_slot[1]]
    w_down = tile_store[tile_slot[2]]
    tok_blocks = inputs.reshape(N_FSDP, TOK_DEV, D)
    cot_blocks = cotangent.reshape(N_FSDP, TOK_DEV, D)

    def visit(carry, pieces):
        output, input_grad, grads = block_pass(pieces[0], pieces[1], w_gate, w_up, w_down, row_index, col_index)
        return carry + grads, (output, input_grad)

    start = jnp.zeros((3, TILES, TILE, TILE), jnp.float32)
    grads, (outputs, input_grads) = lax.scan(visit, start, (tok_blocks, cot_blocks))
    tile_grads = jnp.zeros((N_FSDP * CAP, TILE, TILE), jnp.float32)
    tile_grads = tile_grads.at[tile_slot.reshape(-1)].set(grads.reshape(3 * TILES, TILE, TILE))
    return outputs.reshape(TOKENS, D), input_grads.reshape(TOKENS, D), tile_grads
```

```python
import jax
import jax.numpy as jnp
from jax import lax
from jax.experimental import pallas as pl
from jax.experimental.pallas import tpu as pltpu
from jax.sharding import PartitionSpec as P

BF = jnp.bfloat16
F32 = jnp.float32
VMEM_BYTES = 56 * 1024 * 1024


def dot(a, b, ca, cb):
    return lax.dot_general(a, b, (((ca,), (cb,)), ((), ())), preferred_element_type=F32)


def layer_kernel(
    idx, x, c, store, out, xgrad, grads,
    wgu, wd, gu, dh, hid, dgu, oacc, xacc, sems,
):
    tiles = wd.shape[0]
    side = wd.shape[1]
    row_blocks = oacc.shape[0]

    def fetch(j, carry):
        pltpu.make_async_copy(store.at[idx[2, j]], wgu.at[0, j], sems.at[0]).start()
        pltpu.make_async_copy(store.at[idx[3, j]], wgu.at[1, j], sems.at[0]).start()
        pltpu.make_async_copy(store.at[idx[4, j]], wd.at[j], sems.at[1]).start()
        return carry

    lax.fori_loop(0, tiles, fetch, 0)

    def clear(s, carry):
        grads[s] = jnp.zeros((side, side), BF)
        return carry

    lax.fori_loop(0, grads.shape[0], clear, 0, unroll=8)

    def clear_rows(s, carry):
        oacc[s] = jnp.zeros((side, side), F32)
        xacc[s] = jnp.zeros((side, side), F32)
        return carry

    lax.fori_loop(0, row_blocks, clear_rows, 0, unroll=4)
    pltpu.make_async_copy(wgu, wgu, sems.at[0]).wait()
    pltpu.make_async_copy(wd, wd, sems.at[1]).wait()

    def block(ref, j):
        return ref[:, pl.ds(pl.multiple_of(idx[0, j] * side, side), side)]

    def forward(j, carry):
        k = idx[1, j]
        xj = block(x, j)
        w2 = jnp.concatenate([wgu[0, j], wgu[1, j]], axis=1)
        part = dot(xj, w2, 1, 0)
        dpart = dot(block(c, j), wd[j], 1, 1)
        keep = k != j
        gu[k] = jnp.where(keep, gu[k], 0.0) + part
        dh[k] = jnp.where(keep, dh[k], 0.0) + dpart
        return carry

    lax.fori_loop(0, tiles, forward, 0, unroll=4)

    def gates(j, carry):
        @pl.when(idx[1, j] == j)
        def _():
            gate = gu[j, :, :side]
            up = gu[j, :, side:]
            d = dh[j]
            sig = jax.nn.sigmoid(gate)
            act = gate * sig
            hid[j] = (act * up).astype(BF)
            dgu[j, :, :side] = (d * up * sig * (1.0 + gate * (1.0 - sig))).astype(BF)
            dgu[j, :, side:] = (d * act).astype(BF)

        return carry

    lax.fori_loop(0, tiles, gates, 0)

    def backward(j, carry):
        a = idx[0, j]
        k = idx[1, j]
        h = hid[k]
        d2 = dgu[k]
        xj = block(x, j)
        cj = block(c, j)
        w2 = jnp.concatenate([wgu[0, j], wgu[1, j]], axis=1)
        oacc[a] += dot(h, wd[j], 1, 0)
        xacc[a] += dot(d2, w2, 1, 1)
        g2 = dot(xj, d2, 0, 0).astype(BF)
        grads[idx[2, j]] = g2[:, :side]
        grads[idx[3, j]] = g2[:, side:]
        grads[idx[4, j]] = dot(h, cj, 0, 0).astype(BF)
        return carry

    lax.fori_loop(0, tiles, backward, 0, unroll=4)

    for s in range(row_blocks):
        out[:, s * side:(s + 1) * side] = oacc[s].astype(BF)
        xgrad[:, s * side:(s + 1) * side] = xacc[s].astype(BF)


def layer(idx, x, c, store):
    n_rows, width = x.shape
    slots, side, _ = store.shape
    tiles = idx.shape[1]
    row_blocks = width // side
    vmem = pl.BlockSpec(memory_space=pltpu.VMEM)
    return pl.pallas_call(
        layer_kernel,
        out_shape=(
            jax.ShapeDtypeStruct(x.shape, BF),
            jax.ShapeDtypeStruct(x.shape, BF),
            jax.ShapeDtypeStruct(store.shape, BF),
        ),
        in_specs=[pl.BlockSpec(memory_space=pltpu.SMEM), vmem, vmem, pl.BlockSpec(memory_space=pl.ANY)],
        out_specs=(vmem, vmem, vmem),
        scratch_shapes=[
            pltpu.VMEM((2, tiles, side, side), BF),
            pltpu.VMEM((tiles, side, side), BF),
            pltpu.VMEM((tiles, n_rows, 2 * side), F32),
            pltpu.VMEM((tiles, n_rows, side), F32),
            pltpu.VMEM((tiles, n_rows, side), BF),
            pltpu.VMEM((tiles, n_rows, 2 * side), BF),
            pltpu.VMEM((row_blocks, n_rows, side), F32),
            pltpu.VMEM((row_blocks, n_rows, side), F32),
            pltpu.SemaphoreType.DMA((2,)),
        ],
        compiler_params=pltpu.CompilerParams(vmem_limit_bytes=VMEM_BYTES),
    )(idx, x, c, store)


def on_device(inputs, cotangent, tile_store, pattern, tile_slot):
    cols = pattern[1]
    first = jnp.argmax(cols[:, None] == cols[None, :], axis=1).astype(jnp.int32)
    idx = jnp.concatenate([pattern[:1], first[None], tile_slot], axis=0)
    gathered = lax.all_gather(tile_store, "fsdp", axis=0, tiled=True)
    output, input_grad, grads = layer(idx, inputs, cotangent, gathered)
    tile_grads = lax.psum_scatter(grads, "fsdp", scatter_dimension=0, tiled=True)
    return output, input_grad, tile_grads.astype(F32)


def solution(mesh):
    placed = (
        P(("groups", "fsdp"), None),
        P(("groups", "fsdp"), None),
        P("fsdp", None, None),
        P(),
        P(),
    )
    return jax.shard_map(
        on_device,
        mesh=mesh,
        in_specs=placed,
        out_specs=(
            P(("groups", "fsdp"), None),
            P(("groups", "fsdp"), None),
            P(("groups", "fsdp"), None, None),
        ),
        check_vma=False,
    )
```

```python
import functools

import jax
import jax.numpy as jnp
from jax import lax
from jax.experimental import pallas as pl
from jax.experimental.pallas import tpu as pltpu
from jax.sharding import PartitionSpec as P

BF = jnp.bfloat16
F32 = jnp.float32
VMEM_BYTES = 56 * 1024 * 1024


def dot(a, b, ca, cb):
    return lax.dot_general(a, b, (((ca,), (cb,)), ((), ())), preferred_element_type=F32)


def layer_kernel(
    idx, x, c, store, out, xgrad, left, right,
    wgu, wd, gu, dh, oacc, xacc, sems,
):
    tiles = wd.shape[0]
    side = wd.shape[1]
    row_blocks = oacc.shape[0]

    def fetch(j, carry):
        pltpu.make_async_copy(store.at[idx[2, j]], wgu.at[0, j], sems.at[0]).start()
        pltpu.make_async_copy(store.at[idx[3, j]], wgu.at[1, j], sems.at[0]).start()
        pltpu.make_async_copy(store.at[idx[4, j]], wd.at[j], sems.at[1]).start()
        return carry

    lax.fori_loop(0, tiles, fetch, 0)

    def clear_rows(s, carry):
        oacc[s] = jnp.zeros((side, side), F32)
        xacc[s] = jnp.zeros((side, side), F32)
        return carry

    lax.fori_loop(0, row_blocks, clear_rows, 0, unroll=4)
    pltpu.make_async_copy(wgu, wgu, sems.at[0]).wait()
    pltpu.make_async_copy(wd, wd, sems.at[1]).wait()

    def block(ref, j):
        return ref[:, pl.ds(pl.multiple_of(idx[0, j] * side, side), side)]

    def forward(j, carry):
        k = idx[1, j]
        xj = block(x, j)
        w2 = jnp.concatenate([wgu[0, j], wgu[1, j]], axis=1)
        part = dot(xj, w2, 1, 0)
        dpart = dot(block(c, j), wd[j], 1, 1)
        keep = k != j
        gu[k] = jnp.where(keep, gu[k], 0.0) + part
        dh[k] = jnp.where(keep, dh[k], 0.0) + dpart
        return carry

    lax.fori_loop(0, tiles, forward, 0, unroll=4)

    def gates(j, carry):
        @pl.when(idx[1, j] == j)
        def _():
            gate = gu[j, :, :side]
            up = gu[j, :, side:]
            d = dh[j]
            sig = jax.nn.sigmoid(gate)
            act = gate * sig
            left[row_blocks + j] = (act * up).astype(BF)
            right[j] = (d * up * sig * (1.0 + gate * (1.0 - sig))).astype(BF)
            right[tiles + j] = (d * act).astype(BF)

        return carry

    lax.fori_loop(0, tiles, gates, 0)

    def backward(j, carry):
        a = idx[0, j]
        k = idx[1, j]
        h = left[row_blocks + k]
        d2 = jnp.concatenate([right[k], right[tiles + k]], axis=1)
        w2 = jnp.concatenate([wgu[0, j], wgu[1, j]], axis=1)
        oacc[a] += dot(h, wd[j], 1, 0)
        xacc[a] += dot(d2, w2, 1, 1)
        return carry

    lax.fori_loop(0, tiles, backward, 0, unroll=4)

    left[row_blocks + tiles] = jnp.zeros((x.shape[0], side), BF)
    for s in range(row_blocks):
        left[s] = x[:, s * side:(s + 1) * side]
        right[2 * tiles + s] = c[:, s * side:(s + 1) * side]
        out[:, s * side:(s + 1) * side] = oacc[s].astype(BF)
        xgrad[:, s * side:(s + 1) * side] = xacc[s].astype(BF)


def layer(idx, x, c, store):
    n_rows, width = x.shape
    slots, side, _ = store.shape
    tiles = idx.shape[1]
    row_blocks = width // side
    vmem = pl.BlockSpec(memory_space=pltpu.VMEM)
    return pl.pallas_call(
        layer_kernel,
        out_shape=(
            jax.ShapeDtypeStruct(x.shape, BF),
            jax.ShapeDtypeStruct(x.shape, BF),
            jax.ShapeDtypeStruct((row_blocks + tiles + 1, n_rows, side), BF),
            jax.ShapeDtypeStruct((2 * tiles + row_blocks, n_rows, side), BF),
        ),
        in_specs=[pl.BlockSpec(memory_space=pltpu.SMEM), vmem, vmem, pl.BlockSpec(memory_space=pl.ANY)],
        out_specs=(vmem, vmem, vmem, vmem),
        scratch_shapes=[
            pltpu.VMEM((2, tiles, side, side), BF),
            pltpu.VMEM((tiles, side, side), BF),
            pltpu.VMEM((tiles, n_rows, 2 * side), F32),
            pltpu.VMEM((tiles, n_rows, side), F32),
            pltpu.VMEM((row_blocks, n_rows, side), F32),
            pltpu.VMEM((row_blocks, n_rows, side), F32),
            pltpu.SemaphoreType.DMA((2,)),
        ],
        compiler_params=pltpu.CompilerParams(vmem_limit_bytes=VMEM_BYTES),
    )(idx, x, c, store)


def place():
    me = lax.axis_index("fsdp")
    return me // 4, lax.rem(me // 2, 2), lax.rem(me, 2)


def at(z, y, c):
    return (z * 2 + y) * 2 + c


def greet(partners):
    barrier = pltpu.get_barrier_semaphore()
    for ok, dev in partners:
        if ok is None:
            pl.semaphore_signal(barrier, inc=1, device_id=dev, device_id_type=pl.DeviceIdType.MESH)
        else:
            @pl.when(ok)
            def _():
                pl.semaphore_signal(barrier, inc=1, device_id=dev, device_id_type=pl.DeviceIdType.MESH)
    count = sum(1 if ok is None else ok.astype(jnp.int32) for ok, _ in partners)
    pl.semaphore_wait(barrier, count)


def remote(src, dst, send_sem, recv_sem, dev):
    return pltpu.make_async_remote_copy(
        src_ref=src, dst_ref=dst, send_sem=send_sem, recv_sem=recv_sem,
        device_id=dev, device_id_type=pl.DeviceIdType.MESH,
    )


N_CHUNK = 8
N_BOTH = 2
N_HALF = 3


def gather_kernel(store, full, local_sem, send_sem, recv_sem):
    z, y, c = place()
    g = lax.axis_index("groups")
    cap = store.shape[0]
    size = cap // N_CHUNK
    dev_up = {"fsdp": at(z + 1, y, c)}
    dev_down = {"fsdp": at(z - 1, y, c)}
    dev_y = {"fsdp": at(z, 1 - y, c)}
    dev_x = {"groups": 1 - g}
    dev_core = {"fsdp": at(z, y, 1 - c)}
    greet([(z < 3, dev_up), (z > 0, dev_down), (None, dev_y), (None, dev_x), (None, dev_core)])

    def rows(owner, k):
        return full.at[pl.ds(owner * cap + k * size, size)]

    def copy(way, dev, owner, k, src=None):
        dst = rows(owner, k)
        return remote(dst if src is None else src, dst, send_sem.at[way, owner // 2, k], recv_sem.at[owner, k], dev)

    def send(way, dev, owner, k, act, src=None):
        d = copy(way, dev, owner, k, src)
        d.start() if act else d.wait_send()

    def chunk(i):
        return jnp.where(i < N_BOTH, i, i + g * N_HALF)

    def other(i):
        return N_BOTH + (1 - g) * N_HALF + i

    own = at(z, y, c)
    keep = pltpu.make_async_copy(store, full.at[pl.ds(own * cap, cap)], local_sem)

    def own_sends(act):
        def body(i, carry):
            k = chunk(i)
            src = store.at[pl.ds(k * size, size)]

            @pl.when(z < 3)
            def _():
                send(0, dev_up, own, k, act, src)

            @pl.when(z > 0)
            def _():
                send(1, dev_down, own, k, act, src)

            send(2, dev_y, own, k, act, src)
            return carry

        lax.fori_loop(0, N_BOTH + N_HALF, body, 0)

        def body_core(k, carry):
            send(4, dev_core, own, k, act, store.at[pl.ds(k * size, size)])
            return carry

        lax.fori_loop(0, N_CHUNK, body_core, 0)

    def line(d, act):
        def body(i, carry):
            k = chunk(i)
            for below in (True, False):
                src_z = z - d if below else z + d
                owner = at(src_z, y, c)

                @pl.when((src_z >= 0) if below else (src_z <= 3))
                def _():
                    if act:
                        copy(0, dev_core, owner, k).wait_recv()

                    @pl.when((z < 3) if below else (z > 0))
                    def _():
                        if below:
                            send(0, dev_up, owner, k, act)
                        else:
                            send(1, dev_down, owner, k, act)

                    send(2, dev_y, owner, k, act)

                    @pl.when(i >= N_BOTH)
                    def _():
                        send(3, dev_x, owner, k, act)

                    send(4, dev_core, owner, k, act)

            return carry

        lax.fori_loop(0, N_BOTH + N_HALF, body, 0)

    def across_y(d, act):
        def body(i, carry):
            k = chunk(i)
            for src_z in ((z,) if d == 0 else (z - d, z + d)):
                owner = at(src_z, 1 - y, c)

                @pl.when((src_z >= 0) & (src_z <= 3))
                def _():
                    if act:
                        copy(0, dev_core, owner, k).wait_recv()

                    @pl.when(i >= N_BOTH)
                    def _():
                        send(3, dev_x, owner, k, act)

                    send(4, dev_core, owner, k, act)

            return carry

        lax.fori_loop(0, N_BOTH + N_HALF, body, 0)

    def across_x(d, act):
        def body(i, carry):
            k = other(i)
            for src_z in ((z,) if d == 0 else (z - d, z + d)):
                for yy in ((1 - y,) if d == 0 else (y, 1 - y)):
                    owner = at(src_z, yy, c)

                    @pl.when((src_z >= 0) & (src_z <= 3))
                    def _():
                        if act:
                            copy(0, dev_core, owner, k).wait_recv()
                        send(4, dev_core, owner, k, act)

            return carry

        lax.fori_loop(0, N_HALF, body, 0)

    own_sends(True)
    keep.start()
    steps = ((line, 1), (across_y, 0), (line, 2), (across_y, 1), (across_x, 0), (line, 3), (across_x, 1),
             (across_y, 2), (across_x, 2), (across_y, 3), (across_x, 3))
    for step, d in steps:
        step(d, True)

    def core_in(i, carry):
        owner = (i // N_CHUNK) * 2 + 1 - c
        copy(0, dev_core, owner, lax.rem(i, N_CHUNK)).wait_recv()
        return carry

    lax.fori_loop(0, 8 * N_CHUNK, core_in, 0)
    keep.wait()
    own_sends(False)
    for step, d in steps:
        step(d, False)


def gather_tiles(store):
    cap, side, _ = store.shape
    return pl.pallas_call(
        gather_kernel,
        out_shape=jax.ShapeDtypeStruct((16 * cap, side, side), BF),
        in_specs=[pl.BlockSpec(memory_space=pl.ANY)],
        out_specs=pl.BlockSpec(memory_space=pl.ANY),
        scratch_shapes=[
            pltpu.SemaphoreType.DMA,
            pltpu.SemaphoreType.DMA((5, 8, N_CHUNK)),
            pltpu.SemaphoreType.DMA((16, N_CHUNK)),
        ],
        compiler_params=pltpu.CompilerParams(collective_id=0, has_side_effects=True),
    )(store)


def scatter_kernel(
    lidx, ridx, left, right, out, part, core_in, y_in, lo_in, hi_in,
    core_s, core_r, y_s, y_r, z_s, lo_r, hi_r,
):
    z, y, c = place()
    cap = out.shape[0]
    dev_up = {"fsdp": at(z + 1, y, c)}
    dev_down = {"fsdp": at(z - 1, y, c)}
    dev_y = {"fsdp": at(z, 1 - y, c)}
    dev_core = {"fsdp": at(z, y, 1 - c)}
    greet([(z < 3, dev_up), (z > 0, dev_down), (None, dev_y), (None, dev_core)])

    def order(t):
        base = jnp.where((z == 0) | (z == 3), 3 - t, (3, 0, 2, 1)[t])
        return jnp.where(z >= 2, 3 - base, base)

    def compute(owner):
        def body(i, carry):
            s = owner * cap + i
            part[s] = dot(left[lidx[s]], right[ridx[s]], 0, 0).astype(BF)
            return carry

        lax.fori_loop(0, cap, body, 0, unroll=4)

    def mine(owner):
        return part.at[pl.ds(owner * cap, cap)]

    def core_copy(o, yy):
        return remote(mine(at(o, yy, 1 - c)), core_in.at[o * 2 + yy], core_s.at[o * 2 + yy], core_r.at[o * 2 + yy], dev_core)

    def y_copy(o):
        return remote(mine(at(o, 1 - y, c)), y_in.at[o], y_s.at[o], y_r.at[o], dev_y)

    def up_copy(o):
        return remote(mine(at(o, y, c)), lo_in.at[o], z_s.at[o], lo_r.at[o], dev_up)

    def down_copy(o):
        return remote(mine(at(o, y, c)), hi_in.at[o], z_s.at[o], hi_r.at[o], dev_down)

    def add(owner, terms, final=False):
        def body(i, carry):
            s = owner * cap + i
            total = part[s].astype(F32)
            for ref, slot in terms:
                total += ref[slot, i].astype(F32)
            if final:
                out[i] = total
            else:
                part[s] = total.astype(BF)
            return carry

        lax.fori_loop(0, cap, body, 0, unroll=2)

    for t in range(4):
        o = order(t)
        compute(at(o, 1 - y, 1 - c))
        core_copy(o, 1 - y).start()
    for t in range(4):
        o = order(t)
        compute(at(o, 1 - y, c))
        core_copy(o, 1 - y).wait_recv()
        add(at(o, 1 - y, c), [(core_in, o * 2 + 1 - y)])
        y_copy(o).start()
    for t in range(4):
        o = order(t)
        compute(at(o, y, 1 - c))
        core_copy(o, y).start()
    for t in range(4):
        compute(at(order(t), y, c))
    for t in range(4):
        o = order(t)
        owner = at(o, y, c)
        core_copy(o, y).wait_recv()
        y_copy(o).wait_recv()
        terms = [(core_in, o * 2 + y), (y_in, o)]
        if t < 3:
            @pl.when(o < z)
            def _():
                @pl.when(z < 3)
                def _():
                    down_copy(o).wait_recv()
                    add(owner, terms + [(hi_in, o)])

                @pl.when(z == 3)
                def _():
                    add(owner, terms)

                down_copy(o).start()

            @pl.when(o > z)
            def _():
                @pl.when(z > 0)
                def _():
                    up_copy(o).wait_recv()
                    add(owner, terms + [(lo_in, o)])

                @pl.when(z == 0)
                def _():
                    add(owner, terms)

                up_copy(o).start()
        else:
            @pl.when(z < 3)
            def _():
                down_copy(o).wait_recv()

            @pl.when(z > 0)
            def _():
                up_copy(o).wait_recv()

            @pl.when(z == 0)
            def _():
                add(owner, terms + [(hi_in, o)], True)

            @pl.when(z == 3)
            def _():
                add(owner, terms + [(lo_in, o)], True)

            @pl.when((z > 0) & (z < 3))
            def _():
                add(owner, terms + [(hi_in, o), (lo_in, o)], True)

    for t in range(4):
        o = order(t)
        core_copy(o, y).wait_send()
        core_copy(o, 1 - y).wait_send()
        y_copy(o).wait_send()
        if t < 3:
            up_copy(o).wait_send()


def scatter_grads(lidx, ridx, left, right):
    slots = lidx.shape[0]
    cap = slots // 16
    side = left.shape[2]
    vmem = pl.BlockSpec(memory_space=pltpu.VMEM)
    smem = pl.BlockSpec(memory_space=pltpu.SMEM)
    dma = pltpu.SemaphoreType.DMA
    return pl.pallas_call(
        scatter_kernel,
        out_shape=jax.ShapeDtypeStruct((cap, side, side), F32),
        in_specs=[smem, smem, vmem, vmem],
        out_specs=vmem,
        scratch_shapes=[
            pltpu.VMEM((slots, side, side), BF),
            pltpu.VMEM((8, cap, side, side), BF),
            pltpu.VMEM((4, cap, side, side), BF),
            pltpu.VMEM((4, cap, side, side), BF),
            pltpu.VMEM((4, cap, side, side), BF),
            dma((8,)), dma((8,)), dma((4,)), dma((4,)), dma((4,)), dma((4,)), dma((4,)),
        ],
        compiler_params=pltpu.CompilerParams(
            collective_id=1, has_side_effects=True, vmem_limit_bytes=VMEM_BYTES
        ),
    )(lidx, ridx, left, right)


def grads_kernel(lidx, ridx, left, right, grads):
    def body(s, carry):
        grads[s] = dot(left[lidx[s]], right[ridx[s]], 0, 0).astype(BF)
        return carry

    lax.fori_loop(0, grads.shape[0], body, 0, unroll=4)


def local_grads(lidx, ridx, left, right):
    vmem = pl.BlockSpec(memory_space=pltpu.VMEM)
    smem = pl.BlockSpec(memory_space=pltpu.SMEM)
    side = left.shape[2]
    return pl.pallas_call(
        grads_kernel,
        out_shape=jax.ShapeDtypeStruct((lidx.shape[0], side, side), BF),
        in_specs=[smem, smem, vmem, vmem],
        out_specs=vmem,
        compiler_params=pltpu.CompilerParams(vmem_limit_bytes=VMEM_BYTES),
    )(lidx, ridx, left, right)


def on_device(on_grid, inputs, cotangent, tile_store, pattern, tile_slot):
    tiles = pattern.shape[1]
    row_blocks = inputs.shape[1] // tile_store.shape[1]
    cols = pattern[1]
    first = jnp.argmax(cols[:, None] == cols[None, :], axis=1).astype(jnp.int32)
    idx = jnp.concatenate([pattern[:1], first[None], tile_slot], axis=0)
    slots = tile_store.shape[0] * lax.axis_size("fsdp")
    rows = pattern[0]
    empty = row_blocks + tiles
    pick_l = jnp.concatenate([rows, rows, row_blocks + first]) - empty
    pick_r = jnp.concatenate([first, tiles + first, 2 * tiles + rows])
    hit = jnp.arange(slots, dtype=jnp.int32)[:, None] == tile_slot.reshape(1, -1)
    lidx = jnp.sum(jnp.where(hit, pick_l, 0), axis=1, dtype=jnp.int32) + empty
    ridx = jnp.sum(jnp.where(hit, pick_r, 0), axis=1, dtype=jnp.int32)
    if on_grid:
        gathered = gather_tiles(tile_store)
    else:
        gathered = lax.all_gather(tile_store, "fsdp", axis=0, tiled=True)
    output, input_grad, left, right = layer(idx, inputs, cotangent, gathered)
    if on_grid:
        tile_grads = scatter_grads(lidx, ridx, left, right)
    else:
        grads = local_grads(lidx, ridx, left, right)
        tile_grads = lax.psum_scatter(grads, "fsdp", scatter_dimension=0, tiled=True).astype(F32)
    return output, input_grad, tile_grads


def solution(mesh):
    placed = (
        P(("groups", "fsdp"), None),
        P(("groups", "fsdp"), None),
        P("fsdp", None, None),
        P(),
        P(),
    )
    on_grid = mesh.shape["fsdp"] == 16 and mesh.shape["groups"] == 2
    return jax.shard_map(
        functools.partial(on_device, on_grid),
        mesh=mesh,
        in_specs=placed,
        out_specs=(
            P(("groups", "fsdp"), None),
            P(("groups", "fsdp"), None),
            P(("groups", "fsdp"), None, None),
        ),
        check_vma=False,
    )
```

```python
import functools

import jax
import jax.numpy as jnp
from jax import lax
from jax.experimental import pallas as pl
from jax.experimental.pallas import tpu as pltpu
from jax.sharding import PartitionSpec as P

BF = jnp.bfloat16
F32 = jnp.float32
FF = 14336
VMEM_BYTES = 56 * 1024 * 1024


def dot(a, b, ca, cb):
    return lax.dot_general(a, b, (((ca,), (cb,)), ((), ())), preferred_element_type=F32)


def layer_kernel(
    pattern, slot, x, c, store, out, xgrad, left, right, lidx, ridx,
    first, col_first, wgu, wd, gu, dh, oacc, xacc, sems,
):
    tiles = wd.shape[0]
    side = wd.shape[1]
    row_blocks = oacc.shape[0]

    def fetch(j, carry):
        pltpu.make_async_copy(store.at[slot[0, j]], wgu.at[0, j], sems.at[0]).start()
        pltpu.make_async_copy(store.at[slot[1, j]], wgu.at[1, j], sems.at[0]).start()
        pltpu.make_async_copy(store.at[slot[2, j]], wd.at[j], sems.at[1]).start()
        return carry

    lax.fori_loop(0, tiles, fetch, 0)

    def note_column(i, carry):
        j = tiles - 1 - i
        col_first[pattern[1, j]] = j
        return carry

    lax.fori_loop(0, tiles, note_column, 0, unroll=4)

    def empty_slot(s, carry):
        lidx[s] = row_blocks + tiles
        ridx[s] = 0
        return carry

    lax.fori_loop(0, lidx.shape[0], empty_slot, 0, unroll=8)

    def fill_slot(j, carry):
        a = pattern[0, j]
        k = col_first[pattern[1, j]]
        first[j] = k
        lidx[slot[0, j]] = a
        ridx[slot[0, j]] = k
        lidx[slot[1, j]] = a
        ridx[slot[1, j]] = tiles + k
        lidx[slot[2, j]] = row_blocks + k
        ridx[slot[2, j]] = 2 * tiles + a
        return carry

    lax.fori_loop(0, tiles, fill_slot, 0, unroll=2)

    def clear_rows(s, carry):
        oacc[s] = jnp.zeros((side, side), F32)
        xacc[s] = jnp.zeros((side, side), F32)
        return carry

    lax.fori_loop(0, row_blocks, clear_rows, 0, unroll=4)
    pltpu.make_async_copy(wgu, wgu, sems.at[0]).wait()
    pltpu.make_async_copy(wd, wd, sems.at[1]).wait()

    def block(ref, j):
        return ref[:, pl.ds(pl.multiple_of(pattern[0, j] * side, side), side)]

    def forward(j, carry):
        k = first[j]
        xj = block(x, j)
        w2 = jnp.concatenate([wgu[0, j], wgu[1, j]], axis=1)
        part = dot(xj, w2, 1, 0)
        dpart = dot(block(c, j), wd[j], 1, 1)
        keep = k != j
        gu[k] = jnp.where(keep, gu[k], 0.0) + part
        dh[k] = jnp.where(keep, dh[k], 0.0) + dpart
        return carry

    lax.fori_loop(0, tiles, forward, 0, unroll=4)

    def gates(j, carry):
        @pl.when(first[j] == j)
        def _():
            gate = gu[j, :, :side]
            up = gu[j, :, side:]
            d = dh[j]
            sig = jax.nn.sigmoid(gate)
            act = gate * sig
            left[row_blocks + j] = (act * up).astype(BF)
            right[j] = (d * up * sig * (1.0 + gate * (1.0 - sig))).astype(BF)
            right[tiles + j] = (d * act).astype(BF)

        return carry

    lax.fori_loop(0, tiles, gates, 0)

    def backward(j, carry):
        a = pattern[0, j]
        k = first[j]
        h = left[row_blocks + k]
        d2 = jnp.concatenate([right[k], right[tiles + k]], axis=1)
        w2 = jnp.concatenate([wgu[0, j], wgu[1, j]], axis=1)
        oacc[a] += dot(h, wd[j], 1, 0)
        xacc[a] += dot(d2, w2, 1, 1)
        return carry

    lax.fori_loop(0, tiles, backward, 0, unroll=4)

    left[row_blocks + tiles] = jnp.zeros((x.shape[0], side), BF)
    for s in range(row_blocks):
        left[s] = x[:, s * side:(s + 1) * side]
        right[2 * tiles + s] = c[:, s * side:(s + 1) * side]
        out[:, s * side:(s + 1) * side] = oacc[s].astype(BF)
        xgrad[:, s * side:(s + 1) * side] = xacc[s].astype(BF)


def layer(pattern, slot, x, c, store):
    n_rows, width = x.shape
    slots, side, _ = store.shape
    tiles = pattern.shape[1]
    row_blocks = width // side
    smem = pl.BlockSpec(memory_space=pltpu.SMEM)
    vmem = pl.BlockSpec(memory_space=pltpu.VMEM)
    return pl.pallas_call(
        layer_kernel,
        out_shape=(
            jax.ShapeDtypeStruct(x.shape, BF),
            jax.ShapeDtypeStruct(x.shape, BF),
            jax.ShapeDtypeStruct((row_blocks + tiles + 1, n_rows, side), BF),
            jax.ShapeDtypeStruct((2 * tiles + row_blocks, n_rows, side), BF),
            jax.ShapeDtypeStruct((slots,), jnp.int32),
            jax.ShapeDtypeStruct((slots,), jnp.int32),
        ),
        in_specs=[smem, smem, vmem, vmem, pl.BlockSpec(memory_space=pl.ANY)],
        out_specs=(vmem, vmem, vmem, vmem, smem, smem),
        scratch_shapes=[
            pltpu.SMEM((tiles,), jnp.int32),
            pltpu.SMEM((FF // side,), jnp.int32),
            pltpu.VMEM((2, tiles, side, side), BF),
            pltpu.VMEM((tiles, side, side), BF),
            pltpu.VMEM((tiles, n_rows, 2 * side), F32),
            pltpu.VMEM((tiles, n_rows, side), F32),
            pltpu.VMEM((row_blocks, n_rows, side), F32),
            pltpu.VMEM((row_blocks, n_rows, side), F32),
            pltpu.SemaphoreType.DMA((2,)),
        ],
        compiler_params=pltpu.CompilerParams(vmem_limit_bytes=VMEM_BYTES),
    )(pattern, slot, x, c, store)


def place():
    me = lax.axis_index("fsdp")
    return me // 4, lax.rem(me // 2, 2), lax.rem(me, 2)


def at(z, y, c):
    return (z * 2 + y) * 2 + c


def greet(partners):
    barrier = pltpu.get_barrier_semaphore()
    for ok, dev in partners:
        if ok is None:
            pl.semaphore_signal(barrier, inc=1, device_id=dev, device_id_type=pl.DeviceIdType.MESH)
        else:
            @pl.when(ok)
            def _():
                pl.semaphore_signal(barrier, inc=1, device_id=dev, device_id_type=pl.DeviceIdType.MESH)
    count = sum(1 if ok is None else ok.astype(jnp.int32) for ok, _ in partners)
    pl.semaphore_wait(barrier, count)


def remote(src, dst, send_sem, recv_sem, dev):
    return pltpu.make_async_remote_copy(
        src_ref=src, dst_ref=dst, send_sem=send_sem, recv_sem=recv_sem,
        device_id=dev, device_id_type=pl.DeviceIdType.MESH,
    )


N_CHUNK = 4
N_BOTH = 2
N_HALF = 1


def gather_kernel(store, full, hold, local_sem, send_sem, recv_sem):
    z, y, c = place()
    g = lax.axis_index("groups")
    cap = store.shape[0]
    size = cap // N_CHUNK
    dev_up = {"fsdp": at(z + 1, y, c)}
    dev_down = {"fsdp": at(z - 1, y, c)}
    dev_y = {"fsdp": at(z, 1 - y, c)}
    dev_x = {"groups": 1 - g}
    dev_core = {"fsdp": at(z, y, 1 - c)}
    greet([(z < 3, dev_up), (z > 0, dev_down), (None, dev_y), (None, dev_x), (None, dev_core)])

    def rows(owner, k):
        return full.at[pl.ds(owner * cap + k * size, size)]

    def copy(way, dev, owner, k, src=None):
        dst = rows(owner, k)
        return remote(dst if src is None else src, dst, send_sem.at[way, owner // 2, k], recv_sem.at[owner, k], dev)

    def send(way, dev, owner, k, act, src=None):
        d = copy(way, dev, owner, k, src)
        d.start() if act else d.wait_send()

    def chunk(i):
        return jnp.where(i < N_HALF, N_BOTH + g * N_HALF + i, i - N_HALF)

    def other(i):
        return N_BOTH + (1 - g) * N_HALF + i

    own = at(z, y, c)
    load = pltpu.make_async_copy(store, hold, local_sem.at[0])
    keep = pltpu.make_async_copy(hold, full.at[pl.ds(own * cap, cap)], local_sem.at[1])

    def own_sends(act):
        def body(i, carry):
            k = chunk(i)
            src = store.at[pl.ds(k * size, size)]

            @pl.when(z < 3)
            def _():
                send(0, dev_up, own, k, act, src)

            @pl.when(z > 0)
            def _():
                send(1, dev_down, own, k, act, src)

            send(2, dev_y, own, k, act, src)
            return carry

        lax.fori_loop(0, N_BOTH + N_HALF, body, 0)

        def body_core(k, carry):
            send(4, dev_core, own, k, act, store.at[pl.ds(k * size, size)])
            return carry

        lax.fori_loop(0, N_CHUNK, body_core, 0)

    def line(d, act):
        def body(i, carry):
            k = chunk(i)
            for below in (True, False):
                src_z = z - d if below else z + d
                owner = at(src_z, y, c)

                @pl.when((src_z >= 0) if below else (src_z <= 3))
                def _():
                    if act:
                        copy(0, dev_core, owner, k).wait_recv()

                    @pl.when((z < 3) if below else (z > 0))
                    def _():
                        if below:
                            send(0, dev_up, owner, k, act)
                        else:
                            send(1, dev_down, owner, k, act)

                    send(2, dev_y, owner, k, act)

                    @pl.when(i < N_HALF)
                    def _():
                        send(3, dev_x, owner, k, act)

                    send(4, dev_core, owner, k, act)

            return carry

        lax.fori_loop(0, N_BOTH + N_HALF, body, 0)

    def across_y(d, act):
        def body(i, carry):
            k = chunk(i)
            for src_z in ((z,) if d == 0 else (z - d, z + d)):
                owner = at(src_z, 1 - y, c)

                @pl.when((src_z >= 0) & (src_z <= 3))
                def _():
                    if act:
                        copy(0, dev_core, owner, k).wait_recv()

                    @pl.when(i < N_HALF)
                    def _():
                        send(3, dev_x, owner, k, act)

                    send(4, dev_core, owner, k, act)

            return carry

        lax.fori_loop(0, N_BOTH + N_HALF, body, 0)

    def across_x(d, act):
        def body(i, carry):
            k = other(i)
            for src_z in ((z,) if d == 0 else (z - d, z + d)):
                for yy in ((1 - y,) if d == 0 else (y, 1 - y)):
                    owner = at(src_z, yy, c)

                    @pl.when((src_z >= 0) & (src_z <= 3))
                    def _():
                        if act:
                            copy(0, dev_core, owner, k).wait_recv()
                        send(4, dev_core, owner, k, act)

            return carry

        lax.fori_loop(0, N_HALF, body, 0)

    own_sends(True)
    load.start()
    load.wait()
    keep.start()
    steps = ((line, 1), (across_y, 0), (line, 2), (across_y, 1), (across_x, 0), (line, 3), (across_x, 1),
             (across_y, 2), (across_x, 2), (across_y, 3), (across_x, 3))
    for step, d in steps:
        step(d, True)

    def core_in(i, carry):
        owner = (i // N_CHUNK) * 2 + 1 - c
        copy(0, dev_core, owner, lax.rem(i, N_CHUNK)).wait_recv()
        return carry

    lax.fori_loop(0, 8 * N_CHUNK, core_in, 0)
    keep.wait()
    own_sends(False)
    for step, d in steps:
        step(d, False)


def gather_tiles(store):
    cap, side, _ = store.shape
    return pl.pallas_call(
        gather_kernel,
        out_shape=jax.ShapeDtypeStruct((16 * cap, side, side), BF),
        in_specs=[pl.BlockSpec(memory_space=pl.ANY)],
        out_specs=pl.BlockSpec(memory_space=pl.ANY),
        scratch_shapes=[
            pltpu.VMEM(store.shape, BF),
            pltpu.SemaphoreType.DMA((2,)),
            pltpu.SemaphoreType.DMA((5, 8, N_CHUNK)),
            pltpu.SemaphoreType.DMA((16, N_CHUNK)),
        ],
        compiler_params=pltpu.CompilerParams(collective_id=0, has_side_effects=True),
    )(store)


def scatter_kernel(
    lidx, ridx, left, right, out, part, core_in, y_in, lo_in, hi_in,
    core_s, core_r, y_s, y_r, z_s, lo_r, hi_r,
):
    z, y, c = place()
    cap = out.shape[0]
    dev_up = {"fsdp": at(z + 1, y, c)}
    dev_down = {"fsdp": at(z - 1, y, c)}
    dev_y = {"fsdp": at(z, 1 - y, c)}
    dev_core = {"fsdp": at(z, y, 1 - c)}
    greet([(z < 3, dev_up), (z > 0, dev_down), (None, dev_y), (None, dev_core)])

    def order(t):
        base = jnp.where((z == 0) | (z == 3), 3 - t, (3, 0, 2, 1)[t])
        return jnp.where(z >= 2, 3 - base, base)

    def compute(owner):
        def body(i, carry):
            s = owner * cap + i
            part[s] = dot(left[lidx[s]], right[ridx[s]], 0, 0).astype(BF)
            return carry

        lax.fori_loop(0, cap, body, 0, unroll=4)

    def mine(owner):
        return part.at[pl.ds(owner * cap, cap)]

    def core_copy(o, yy):
        return remote(mine(at(o, yy, 1 - c)), core_in.at[o * 2 + yy], core_s.at[o * 2 + yy], core_r.at[o * 2 + yy], dev_core)

    def y_copy(o):
        return remote(mine(at(o, 1 - y, c)), y_in.at[o], y_s.at[o], y_r.at[o], dev_y)

    def up_copy(o):
        return remote(mine(at(o, y, c)), lo_in.at[o], z_s.at[o], lo_r.at[o], dev_up)

    def down_copy(o):
        return remote(mine(at(o, y, c)), hi_in.at[o], z_s.at[o], hi_r.at[o], dev_down)

    def add(owner, terms, final=False):
        def body(i, carry):
            s = owner * cap + i
            total = part[s].astype(F32)
            for ref, slot in terms:
                total += ref[slot, i].astype(F32)
            if final:
                out[i] = total
            else:
                part[s] = total.astype(BF)
            return carry

        lax.fori_loop(0, cap, body, 0, unroll=2)

    def to_core(o):
        compute(at(o, 1 - y, 1 - c))
        core_copy(o, 1 - y).start()

    def to_y(o):
        compute(at(o, 1 - y, c))
        core_copy(o, 1 - y).wait_recv()
        add(at(o, 1 - y, c), [(core_in, o * 2 + 1 - y)])
        y_copy(o).start()

    to_core(order(0))
    for t in range(4):
        if t < 3:
            to_core(order(t + 1))
        to_y(order(t))
    for t in range(4):
        o = order(t)
        compute(at(o, y, 1 - c))
        core_copy(o, y).start()
    for t in range(4):
        compute(at(order(t), y, c))
    for t in range(4):
        o = order(t)
        owner = at(o, y, c)
        core_copy(o, y).wait_recv()
        y_copy(o).wait_recv()
        terms = [(core_in, o * 2 + y), (y_in, o)]
        if t < 3:
            @pl.when(o < z)
            def _():
                @pl.when(z < 3)
                def _():
                    down_copy(o).wait_recv()
                    add(owner, terms + [(hi_in, o)])

                @pl.when(z == 3)
                def _():
                    add(owner, terms)

                down_copy(o).start()

            @pl.when(o > z)
            def _():
                @pl.when(z > 0)
                def _():
                    up_copy(o).wait_recv()
                    add(owner, terms + [(lo_in, o)])

                @pl.when(z == 0)
                def _():
                    add(owner, terms)

                up_copy(o).start()
        else:
            @pl.when(z < 3)
            def _():
                down_copy(o).wait_recv()

            @pl.when(z > 0)
            def _():
                up_copy(o).wait_recv()

            @pl.when(z == 0)
            def _():
                add(owner, terms + [(hi_in, o)], True)

            @pl.when(z == 3)
            def _():
                add(owner, terms + [(lo_in, o)], True)

            @pl.when((z > 0) & (z < 3))
            def _():
                add(owner, terms + [(hi_in, o), (lo_in, o)], True)

    for t in range(4):
        o = order(t)
        core_copy(o, y).wait_send()
        core_copy(o, 1 - y).wait_send()
        y_copy(o).wait_send()
        if t < 3:
            up_copy(o).wait_send()


def scatter_grads(lidx, ridx, left, right):
    slots = lidx.shape[0]
    cap = slots // 16
    side = left.shape[2]
    vmem = pl.BlockSpec(memory_space=pltpu.VMEM)
    smem = pl.BlockSpec(memory_space=pltpu.SMEM)
    dma = pltpu.SemaphoreType.DMA
    return pl.pallas_call(
        scatter_kernel,
        out_shape=jax.ShapeDtypeStruct((cap, side, side), F32),
        in_specs=[smem, smem, vmem, vmem],
        out_specs=vmem,
        scratch_shapes=[
            pltpu.VMEM((slots, side, side), BF),
            pltpu.VMEM((8, cap, side, side), BF),
            pltpu.VMEM((4, cap, side, side), BF),
            pltpu.VMEM((4, cap, side, side), BF),
            pltpu.VMEM((4, cap, side, side), BF),
            dma((8,)), dma((8,)), dma((4,)), dma((4,)), dma((4,)), dma((4,)), dma((4,)),
        ],
        compiler_params=pltpu.CompilerParams(
            collective_id=1, has_side_effects=True, vmem_limit_bytes=VMEM_BYTES
        ),
    )(lidx, ridx, left, right)


def grads_kernel(lidx, ridx, left, right, grads):
    def body(s, carry):
        grads[s] = dot(left[lidx[s]], right[ridx[s]], 0, 0).astype(BF)
        return carry

    lax.fori_loop(0, grads.shape[0], body, 0, unroll=4)


def local_grads(lidx, ridx, left, right):
    vmem = pl.BlockSpec(memory_space=pltpu.VMEM)
    smem = pl.BlockSpec(memory_space=pltpu.SMEM)
    side = left.shape[2]
    return pl.pallas_call(
        grads_kernel,
        out_shape=jax.ShapeDtypeStruct((lidx.shape[0], side, side), BF),
        in_specs=[smem, smem, vmem, vmem],
        out_specs=vmem,
        compiler_params=pltpu.CompilerParams(vmem_limit_bytes=VMEM_BYTES),
    )(lidx, ridx, left, right)


def on_device(on_grid, inputs, cotangent, tile_store, pattern, tile_slot):
    if on_grid:
        gathered = gather_tiles(tile_store)
    else:
        gathered = lax.all_gather(tile_store, "fsdp", axis=0, tiled=True)
    output, input_grad, left, right, lidx, ridx = layer(pattern, tile_slot, inputs, cotangent, gathered)
    if on_grid:
        tile_grads = scatter_grads(lidx, ridx, left, right)
    else:
        grads = local_grads(lidx, ridx, left, right)
        tile_grads = lax.psum_scatter(grads, "fsdp", scatter_dimension=0, tiled=True).astype(F32)
    return output, input_grad, tile_grads


def solution(mesh):
    placed = (
        P(("groups", "fsdp"), None),
        P(("groups", "fsdp"), None),
        P("fsdp", None, None),
        P(),
        P(),
    )
    on_grid = mesh.shape["fsdp"] == 16 and mesh.shape["groups"] == 2
    return jax.shard_map(
        functools.partial(on_device, on_grid),
        mesh=mesh,
        in_specs=placed,
        out_specs=(
            P(("groups", "fsdp"), None),
            P(("groups", "fsdp"), None),
            P(("groups", "fsdp"), None, None),
        ),
        check_vma=False,
    )
```

```python
import functools

import jax
import jax.numpy as jnp
from jax import lax
from jax.experimental import pallas as pl
from jax.experimental.pallas import tpu as pltpu
from jax.sharding import PartitionSpec as P

BF = jnp.bfloat16
F32 = jnp.float32
FF = 14336
VMEM_BYTES = 56 * 1024 * 1024


def dot(a, b, ca, cb):
    return lax.dot_general(a, b, (((ca,), (cb,)), ((), ())), preferred_element_type=F32)


def layer_kernel(
    pattern, slot, x, c, store, out, xgrad, left, right, lidx, ridx,
    first, col_first, wgu, wd, gu, dh, oacc, xacc, sems,
):
    tiles = wd.shape[0]
    side = wd.shape[1]
    row_blocks = oacc.shape[0]

    def fetch(j, carry):
        pltpu.make_async_copy(store.at[slot[0, j]], wgu.at[0, j], sems.at[0]).start()
        pltpu.make_async_copy(store.at[slot[1, j]], wgu.at[1, j], sems.at[0]).start()
        pltpu.make_async_copy(store.at[slot[2, j]], wd.at[j], sems.at[1]).start()
        return carry

    lax.fori_loop(0, tiles, fetch, 0)

    def note_column(i, carry):
        j = tiles - 1 - i
        col_first[pattern[1, j]] = j
        return carry

    lax.fori_loop(0, tiles, note_column, 0, unroll=4)

    def empty_slot(s, carry):
        lidx[s] = row_blocks + tiles
        ridx[s] = 0
        return carry

    lax.fori_loop(0, lidx.shape[0], empty_slot, 0, unroll=8)

    def fill_slot(j, carry):
        a = pattern[0, j]
        k = col_first[pattern[1, j]]
        first[j] = k
        lidx[slot[0, j]] = a
        ridx[slot[0, j]] = k
        lidx[slot[1, j]] = a
        ridx[slot[1, j]] = tiles + k
        lidx[slot[2, j]] = row_blocks + k
        ridx[slot[2, j]] = 2 * tiles + a
        return carry

    lax.fori_loop(0, tiles, fill_slot, 0, unroll=2)

    def clear_rows(s, carry):
        oacc[s] = jnp.zeros((side, side), F32)
        xacc[s] = jnp.zeros((side, side), F32)
        return carry

    lax.fori_loop(0, row_blocks, clear_rows, 0, unroll=4)
    pltpu.make_async_copy(wgu, wgu, sems.at[0]).wait()
    pltpu.make_async_copy(wd, wd, sems.at[1]).wait()

    def block(ref, j):
        return ref[:, pl.ds(pl.multiple_of(pattern[0, j] * side, side), side)]

    def forward(j, carry):
        k = first[j]
        xj = block(x, j)
        w2 = jnp.concatenate([wgu[0, j], wgu[1, j]], axis=1)
        part = dot(xj, w2, 1, 0)
        dpart = dot(block(c, j), wd[j], 1, 1)
        keep = k != j
        gu[k] = jnp.where(keep, gu[k], 0.0) + part
        dh[k] = jnp.where(keep, dh[k], 0.0) + dpart
        return carry

    lax.fori_loop(0, tiles, forward, 0, unroll=4)

    def gates(j, carry):
        @pl.when(first[j] == j)
        def _():
            gate = gu[j, :, :side]
            up = gu[j, :, side:]
            d = dh[j]
            sig = jax.nn.sigmoid(gate)
            act = gate * sig
            left[row_blocks + j] = (act * up).astype(BF)
            right[j] = (d * up * sig * (1.0 + gate * (1.0 - sig))).astype(BF)
            right[tiles + j] = (d * act).astype(BF)

        return carry

    lax.fori_loop(0, tiles, gates, 0)

    def backward(j, carry):
        a = pattern[0, j]
        k = first[j]
        h = left[row_blocks + k]
        d2 = jnp.concatenate([right[k], right[tiles + k]], axis=1)
        w2 = jnp.concatenate([wgu[0, j], wgu[1, j]], axis=1)
        oacc[a] += dot(h, wd[j], 1, 0)
        xacc[a] += dot(d2, w2, 1, 1)
        return carry

    lax.fori_loop(0, tiles, backward, 0, unroll=4)

    left[row_blocks + tiles] = jnp.zeros((x.shape[0], side), BF)
    for s in range(row_blocks):
        left[s] = x[:, s * side:(s + 1) * side]
        right[2 * tiles + s] = c[:, s * side:(s + 1) * side]
        out[:, s * side:(s + 1) * side] = oacc[s].astype(BF)
        xgrad[:, s * side:(s + 1) * side] = xacc[s].astype(BF)


def layer(pattern, slot, x, c, store):
    n_rows, width = x.shape
    slots, side, _ = store.shape
    tiles = pattern.shape[1]
    row_blocks = width // side
    smem = pl.BlockSpec(memory_space=pltpu.SMEM)
    vmem = pl.BlockSpec(memory_space=pltpu.VMEM)
    return pl.pallas_call(
        layer_kernel,
        out_shape=(
            jax.ShapeDtypeStruct(x.shape, BF),
            jax.ShapeDtypeStruct(x.shape, BF),
            jax.ShapeDtypeStruct((row_blocks + tiles + 1, n_rows, side), BF),
            jax.ShapeDtypeStruct((2 * tiles + row_blocks, n_rows, side), BF),
            jax.ShapeDtypeStruct((slots,), jnp.int32),
            jax.ShapeDtypeStruct((slots,), jnp.int32),
        ),
        in_specs=[smem, smem, vmem, vmem, pl.BlockSpec(memory_space=pl.ANY)],
        out_specs=(vmem, vmem, vmem, vmem, smem, smem),
        scratch_shapes=[
            pltpu.SMEM((tiles,), jnp.int32),
            pltpu.SMEM((FF // side,), jnp.int32),
            pltpu.VMEM((2, tiles, side, side), BF),
            pltpu.VMEM((tiles, side, side), BF),
            pltpu.VMEM((tiles, n_rows, 2 * side), F32),
            pltpu.VMEM((tiles, n_rows, side), F32),
            pltpu.VMEM((row_blocks, n_rows, side), F32),
            pltpu.VMEM((row_blocks, n_rows, side), F32),
            pltpu.SemaphoreType.DMA((2,)),
        ],
        compiler_params=pltpu.CompilerParams(vmem_limit_bytes=VMEM_BYTES),
    )(pattern, slot, x, c, store)


def place():
    me = lax.axis_index("fsdp")
    return me // 4, lax.rem(me // 2, 2), lax.rem(me, 2)


def at(z, y, c):
    return (z * 2 + y) * 2 + c


def greet(partners):
    barrier = pltpu.get_barrier_semaphore()
    for ok, dev in partners:
        if ok is None:
            pl.semaphore_signal(barrier, inc=1, device_id=dev, device_id_type=pl.DeviceIdType.MESH)
        else:
            @pl.when(ok)
            def _():
                pl.semaphore_signal(barrier, inc=1, device_id=dev, device_id_type=pl.DeviceIdType.MESH)
    count = sum(1 if ok is None else ok.astype(jnp.int32) for ok, _ in partners)
    pl.semaphore_wait(barrier, count)


def remote(src, dst, send_sem, recv_sem, dev):
    return pltpu.make_async_remote_copy(
        src_ref=src, dst_ref=dst, send_sem=send_sem, recv_sem=recv_sem,
        device_id=dev, device_id_type=pl.DeviceIdType.MESH,
    )


N_CHUNK = 4
N_BOTH = 2
N_HALF = 1


def gather_kernel(store, full, hold, local_sem, send_sem, recv_sem):
    z, y, c = place()
    g = lax.axis_index("groups")
    cap = store.shape[0]
    size = cap // N_CHUNK
    dev_up = {"fsdp": at(z + 1, y, c)}
    dev_down = {"fsdp": at(z - 1, y, c)}
    dev_y = {"fsdp": at(z, 1 - y, c)}
    dev_x = {"groups": 1 - g}
    dev_core = {"fsdp": at(z, y, 1 - c)}
    greet([(z < 3, dev_up), (z > 0, dev_down), (None, dev_y), (None, dev_x), (None, dev_core)])

    def rows(owner, k):
        return full.at[pl.ds(owner * cap + k * size, size)]

    def copy(way, dev, owner, k, src=None):
        dst = rows(owner, k)
        return remote(dst if src is None else src, dst, send_sem.at[way, owner // 2, k], recv_sem.at[owner, k], dev)

    def send(way, dev, owner, k, act, src=None):
        d = copy(way, dev, owner, k, src)
        d.start() if act else d.wait_send()

    def chunk(i):
        return jnp.where(i < N_HALF, N_BOTH + g * N_HALF + i, i - N_HALF)

    def other(i):
        return N_BOTH + (1 - g) * N_HALF + i

    own = at(z, y, c)
    load = pltpu.make_async_copy(store, hold, local_sem.at[0])
    keep = pltpu.make_async_copy(hold, full.at[pl.ds(own * cap, cap)], local_sem.at[1])

    def own_sends(act):
        def body(i, carry):
            k = chunk(i)
            src = store.at[pl.ds(k * size, size)]

            @pl.when(z < 3)
            def _():
                send(0, dev_up, own, k, act, src)

            @pl.when(z > 0)
            def _():
                send(1, dev_down, own, k, act, src)

            send(2, dev_y, own, k, act, src)
            return carry

        lax.fori_loop(0, N_BOTH + N_HALF, body, 0)

        def body_core(k, carry):
            send(4, dev_core, own, k, act, store.at[pl.ds(k * size, size)])
            return carry

        lax.fori_loop(0, N_CHUNK, body_core, 0)

    def line(d, act):
        def body(i, carry):
            k = chunk(i)
            for below in (True, False):
                src_z = z - d if below else z + d
                owner = at(src_z, y, c)

                @pl.when((src_z >= 0) if below else (src_z <= 3))
                def _():
                    if act:
                        copy(0, dev_core, owner, k).wait_recv()

                    @pl.when((z < 3) if below else (z > 0))
                    def _():
                        if below:
                            send(0, dev_up, owner, k, act)
                        else:
                            send(1, dev_down, owner, k, act)

                    send(2, dev_y, owner, k, act)

                    @pl.when(i < N_HALF)
                    def _():
                        send(3, dev_x, owner, k, act)

                    send(4, dev_core, owner, k, act)

            return carry

        lax.fori_loop(0, N_BOTH + N_HALF, body, 0)

    def across_y(d, act):
        def body(i, carry):
            k = chunk(i)
            for src_z in ((z,) if d == 0 else (z - d, z + d)):
                owner = at(src_z, 1 - y, c)

                @pl.when((src_z >= 0) & (src_z <= 3))
                def _():
                    if act:
                        copy(0, dev_core, owner, k).wait_recv()

                    @pl.when(i < N_HALF)
                    def _():
                        send(3, dev_x, owner, k, act)

                    send(4, dev_core, owner, k, act)

            return carry

        lax.fori_loop(0, N_BOTH + N_HALF, body, 0)

    def across_x(d, act):
        def body(i, carry):
            k = other(i)
            for src_z in ((z,) if d == 0 else (z - d, z + d)):
                for yy in ((1 - y,) if d == 0 else (y, 1 - y)):
                    owner = at(src_z, yy, c)

                    @pl.when((src_z >= 0) & (src_z <= 3))
                    def _():
                        if act:
                            copy(0, dev_core, owner, k).wait_recv()
                        send(4, dev_core, owner, k, act)

            return carry

        lax.fori_loop(0, N_HALF, body, 0)

    own_sends(True)
    load.start()
    load.wait()
    keep.start()
    steps = ((line, 1), (across_y, 0), (line, 2), (across_y, 1), (across_x, 0), (line, 3), (across_x, 1),
             (across_y, 2), (across_x, 2), (across_y, 3), (across_x, 3))
    for step, d in steps:
        step(d, True)

    def core_in(i, carry):
        owner = (i // N_CHUNK) * 2 + 1 - c
        copy(0, dev_core, owner, lax.rem(i, N_CHUNK)).wait_recv()
        return carry

    lax.fori_loop(0, 8 * N_CHUNK, core_in, 0)
    keep.wait()
    own_sends(False)
    for step, d in steps:
        step(d, False)


def gather_tiles(store):
    cap, side, _ = store.shape
    return pl.pallas_call(
        gather_kernel,
        out_shape=jax.ShapeDtypeStruct((16 * cap, side, side), BF),
        in_specs=[pl.BlockSpec(memory_space=pl.ANY)],
        out_specs=pl.BlockSpec(memory_space=pl.ANY),
        scratch_shapes=[
            pltpu.VMEM(store.shape, BF),
            pltpu.SemaphoreType.DMA((2,)),
            pltpu.SemaphoreType.DMA((5, 8, N_CHUNK)),
            pltpu.SemaphoreType.DMA((16, N_CHUNK)),
        ],
        compiler_params=pltpu.CompilerParams(collective_id=0, has_side_effects=True),
    )(store)


def scatter_kernel(
    lidx, ridx, left, right, out, part, core_in, y_in, lo_in, hi_in, far_lo, far_hi, far_y,
    core_s, core_r, y_s, y_r, z_s, lo_r, hi_r, far_s, far_lo_r, far_hi_r, far_y_sem,
):
    z, y, c = place()
    cap = out.shape[0]
    few = far_y.shape[0]
    dev_up = {"fsdp": at(z + 1, y, c)}
    dev_down = {"fsdp": at(z - 1, y, c)}
    dev_y = {"fsdp": at(z, 1 - y, c)}
    dev_core = {"fsdp": at(z, y, 1 - c)}
    greet([(z < 3, dev_up), (z > 0, dev_down), (None, dev_y), (None, dev_core)])

    def order(t):
        base = jnp.where((z == 0) | (z == 3), 3 - t, (3, 0, 2, 1)[t])
        return jnp.where(z >= 2, 3 - base, base)

    def compute(owner):
        def body(i, carry):
            s = owner * cap + i
            part[s] = dot(left[lidx[s]], right[ridx[s]], 0, 0).astype(BF)
            return carry

        lax.fori_loop(0, cap, body, 0, unroll=4)

    def mine(owner):
        return part.at[pl.ds(owner * cap, cap)]

    def core_copy(o, yy):
        return remote(mine(at(o, yy, 1 - c)), core_in.at[o * 2 + yy], core_s.at[o * 2 + yy], core_r.at[o * 2 + yy], dev_core)

    def y_copy(o):
        rest = pl.ds(at(o, 1 - y, c) * cap + few, cap - few)
        return remote(part.at[rest], y_in.at[o, pl.ds(few, cap - few)], y_s.at[o], y_r.at[o], dev_y)

    def up_copy(o):
        return remote(mine(at(o, y, c)), lo_in.at[o], z_s.at[o], lo_r.at[o], dev_up)

    def down_copy(o):
        return remote(mine(at(o, y, c)), hi_in.at[o], z_s.at[o], hi_r.at[o], dev_down)

    def far_rows(o):
        return part.at[pl.ds(at(o, 1 - y, c) * cap, few)]

    def far_up(o):
        return remote(far_rows(o), far_lo.at[o], far_s.at[o], far_lo_r.at[o], dev_up)

    def far_down(o):
        return remote(far_rows(o), far_hi.at[o], far_s.at[o], far_hi_r.at[o], dev_down)

    def far_y_copy():
        return remote(far_rows(z), far_y, far_y_sem.at[0], far_y_sem.at[1], dev_y)

    def add(owner, terms, start, stop, final=False):
        def body(i, carry):
            s = owner * cap + i
            total = part[s].astype(F32)
            for get in terms:
                total += get(i).astype(F32)
            if final:
                out[i] = total
            else:
                part[s] = total.astype(BF)
            return carry

        lax.fori_loop(start, stop, body, 0, unroll=2)

    def chain(t, o, up, down, lo, hi, total):
        if t < 3:
            @pl.when(o < z)
            def _():
                @pl.when(z < 3)
                def _():
                    down(o).wait_recv()
                    total([lambda i: hi[o, i]])

                @pl.when(z == 3)
                def _():
                    total([])

                down(o).start()

            @pl.when(o > z)
            def _():
                @pl.when(z > 0)
                def _():
                    up(o).wait_recv()
                    total([lambda i: lo[o, i]])

                @pl.when(z == 0)
                def _():
                    total([])

                up(o).start()
        else:
            @pl.when(z < 3)
            def _():
                down(o).wait_recv()

            @pl.when(z > 0)
            def _():
                up(o).wait_recv()

            @pl.when(z == 0)
            def _():
                total([lambda i: hi[o, i]])

            @pl.when(z == 3)
            def _():
                total([lambda i: lo[o, i]])

            @pl.when((z > 0) & (z < 3))
            def _():
                total([lambda i: hi[o, i], lambda i: lo[o, i]])

    def to_core(o):
        compute(at(o, 1 - y, 1 - c))
        core_copy(o, 1 - y).start()

    def to_y(o):
        compute(at(o, 1 - y, c))
        core_copy(o, 1 - y).wait_recv()
        add(at(o, 1 - y, c), [lambda i: core_in[o * 2 + 1 - y, i]], few, cap)
        y_copy(o).start()

    to_core(order(0))
    for t in range(4):
        if t < 3:
            to_core(order(t + 1))
        to_y(order(t))
    for t in range(4):
        o = order(t)
        compute(at(o, y, 1 - c))
        core_copy(o, y).start()
    for t in range(4):
        compute(at(order(t), y, c))
    def far_step(t, o):
        def total(terms):
            add(at(o, 1 - y, c), [lambda i: core_in[o * 2 + 1 - y, i]] + terms, 0, few)

        chain(t, o, far_up, far_down, far_lo, far_hi, total)

    def near_step(t, o):
        final = t == 3
        core_copy(o, y).wait_recv()
        y_copy(o).wait_recv()
        if final:
            far_y_copy().wait_recv()

        def total(terms):
            terms = [lambda i: core_in[o * 2 + y, i]] + terms
            add(at(o, y, c), terms + ([lambda i: far_y[i]] if final else []), 0, few, final)
            add(at(o, y, c), terms + [lambda i: y_in[o, i]], few, cap, final)

        chain(t, o, up_copy, down_copy, lo_in, hi_in, total)

    for t in range(4):
        far_step(t, order(t))
    far_y_copy().start()
    for t in range(4):
        near_step(t, order(t))
    for t in range(4):
        o = order(t)
        core_copy(o, y).wait_send()
        core_copy(o, 1 - y).wait_send()
        y_copy(o).wait_send()
        if t < 3:
            up_copy(o).wait_send()
            far_up(o).wait_send()
    far_y_copy().wait_send()


def scatter_grads(lidx, ridx, left, right):
    slots = lidx.shape[0]
    cap = slots // 16
    few = 3 * cap // 16
    side = left.shape[2]
    vmem = pl.BlockSpec(memory_space=pltpu.VMEM)
    smem = pl.BlockSpec(memory_space=pltpu.SMEM)
    dma = pltpu.SemaphoreType.DMA
    return pl.pallas_call(
        scatter_kernel,
        out_shape=jax.ShapeDtypeStruct((cap, side, side), F32),
        in_specs=[smem, smem, vmem, vmem],
        out_specs=vmem,
        scratch_shapes=[
            pltpu.VMEM((slots, side, side), BF),
            pltpu.VMEM((8, cap, side, side), BF),
            pltpu.VMEM((4, cap, side, side), BF),
            pltpu.VMEM((4, cap, side, side), BF),
            pltpu.VMEM((4, cap, side, side), BF),
            pltpu.VMEM((4, few, side, side), BF),
            pltpu.VMEM((4, few, side, side), BF),
            pltpu.VMEM((few, side, side), BF),
            dma((8,)), dma((8,)), dma((4,)), dma((4,)), dma((4,)), dma((4,)), dma((4,)),
            dma((4,)), dma((4,)), dma((4,)), dma((2,)),
        ],
        compiler_params=pltpu.CompilerParams(
            collective_id=1, has_side_effects=True, vmem_limit_bytes=VMEM_BYTES
        ),
    )(lidx, ridx, left, right)


def grads_kernel(lidx, ridx, left, right, grads):
    def body(s, carry):
        grads[s] = dot(left[lidx[s]], right[ridx[s]], 0, 0).astype(BF)
        return carry

    lax.fori_loop(0, grads.shape[0], body, 0, unroll=4)


def local_grads(lidx, ridx, left, right):
    vmem = pl.BlockSpec(memory_space=pltpu.VMEM)
    smem = pl.BlockSpec(memory_space=pltpu.SMEM)
    side = left.shape[2]
    return pl.pallas_call(
        grads_kernel,
        out_shape=jax.ShapeDtypeStruct((lidx.shape[0], side, side), BF),
        in_specs=[smem, smem, vmem, vmem],
        out_specs=vmem,
        compiler_params=pltpu.CompilerParams(vmem_limit_bytes=VMEM_BYTES),
    )(lidx, ridx, left, right)


def on_device(on_grid, inputs, cotangent, tile_store, pattern, tile_slot):
    if on_grid:
        gathered = gather_tiles(tile_store)
    else:
        gathered = lax.all_gather(tile_store, "fsdp", axis=0, tiled=True)
    output, input_grad, left, right, lidx, ridx = layer(pattern, tile_slot, inputs, cotangent, gathered)
    if on_grid:
        tile_grads = scatter_grads(lidx, ridx, left, right)
    else:
        grads = local_grads(lidx, ridx, left, right)
        tile_grads = lax.psum_scatter(grads, "fsdp", scatter_dimension=0, tiled=True).astype(F32)
    return output, input_grad, tile_grads


def solution(mesh):
    placed = (
        P(("groups", "fsdp"), None),
        P(("groups", "fsdp"), None),
        P("fsdp", None, None),
        P(),
        P(),
    )
    on_grid = mesh.shape["fsdp"] == 16 and mesh.shape["groups"] == 2
    return jax.shard_map(
        functools.partial(on_device, on_grid),
        mesh=mesh,
        in_specs=placed,
        out_specs=(
            P(("groups", "fsdp"), None),
            P(("groups", "fsdp"), None),
            P(("groups", "fsdp"), None, None),
        ),
        check_vma=False,
    )
```

```python
import functools

import jax
import jax.numpy as jnp
from jax import lax
from jax.experimental import pallas as pl
from jax.experimental.pallas import tpu as pltpu
from jax.sharding import PartitionSpec as P

BF = jnp.bfloat16
F32 = jnp.float32
FF = 14336
VMEM_BYTES = 56 * 1024 * 1024


def dot(a, b, ca, cb):
    return lax.dot_general(a, b, (((ca,), (cb,)), ((), ())), preferred_element_type=F32)


def layer_kernel(
    pattern, slot, x, c, store, out, xgrad, left, right, lidx, ridx,
    first, col_first, wgu, wd, gu, dh, oacc, xacc, sems,
):
    tiles = wd.shape[0]
    side = wd.shape[1]
    row_blocks = oacc.shape[0]

    def fetch(j, carry):
        pltpu.make_async_copy(store.at[slot[0, j]], wgu.at[0, j], sems.at[0]).start()
        pltpu.make_async_copy(store.at[slot[1, j]], wgu.at[1, j], sems.at[0]).start()
        pltpu.make_async_copy(store.at[slot[2, j]], wd.at[j], sems.at[1]).start()
        return carry

    lax.fori_loop(0, tiles, fetch, 0)

    def note_column(i, carry):
        j = tiles - 1 - i
        col_first[pattern[1, j]] = j
        return carry

    lax.fori_loop(0, tiles, note_column, 0, unroll=4)

    def empty_slot(s, carry):
        lidx[s] = row_blocks + tiles
        ridx[s] = 0
        return carry

    lax.fori_loop(0, lidx.shape[0], empty_slot, 0, unroll=8)

    def fill_slot(j, carry):
        a = pattern[0, j]
        k = col_first[pattern[1, j]]
        first[j] = k
        lidx[slot[0, j]] = a
        ridx[slot[0, j]] = k
        lidx[slot[1, j]] = a
        ridx[slot[1, j]] = tiles + k
        lidx[slot[2, j]] = row_blocks + k
        ridx[slot[2, j]] = 2 * tiles + a
        return carry

    lax.fori_loop(0, tiles, fill_slot, 0, unroll=2)

    def clear_rows(s, carry):
        oacc[s] = jnp.zeros((side, side), F32)
        xacc[s] = jnp.zeros((side, side), F32)
        return carry

    lax.fori_loop(0, row_blocks, clear_rows, 0, unroll=4)
    pltpu.make_async_copy(wgu, wgu, sems.at[0]).wait()
    pltpu.make_async_copy(wd, wd, sems.at[1]).wait()

    def block(ref, j):
        return ref[:, pl.ds(pl.multiple_of(pattern[0, j] * side, side), side)]

    def forward(j, carry):
        k = first[j]
        xj = block(x, j)
        w2 = jnp.concatenate([wgu[0, j], wgu[1, j]], axis=1)
        part = dot(xj, w2, 1, 0)
        dpart = dot(block(c, j), wd[j], 1, 1)
        keep = k != j
        gu[k] = jnp.where(keep, gu[k], 0.0) + part
        dh[k] = jnp.where(keep, dh[k], 0.0) + dpart
        return carry

    lax.fori_loop(0, tiles, forward, 0, unroll=4)

    def gates(j, carry):
        @pl.when(first[j] == j)
        def _():
            gate = gu[j, :, :side]
            up = gu[j, :, side:]
            d = dh[j]
            sig = jax.nn.sigmoid(gate)
            act = gate * sig
            left[row_blocks + j] = (act * up).astype(BF)
            right[j] = (d * up * sig * (1.0 + gate * (1.0 - sig))).astype(BF)
            right[tiles + j] = (d * act).astype(BF)

        return carry

    lax.fori_loop(0, tiles, gates, 0)

    def backward(j, carry):
        a = pattern[0, j]
        k = first[j]
        h = left[row_blocks + k]
        d2 = jnp.concatenate([right[k], right[tiles + k]], axis=1)
        w2 = jnp.concatenate([wgu[0, j], wgu[1, j]], axis=1)
        oacc[a] += dot(h, wd[j], 1, 0)
        xacc[a] += dot(d2, w2, 1, 1)
        return carry

    lax.fori_loop(0, tiles, backward, 0, unroll=4)

    left[row_blocks + tiles] = jnp.zeros((x.shape[0], side), BF)
    for s in range(row_blocks):
        left[s] = x[:, s * side:(s + 1) * side]
        right[2 * tiles + s] = c[:, s * side:(s + 1) * side]
        out[:, s * side:(s + 1) * side] = oacc[s].astype(BF)
        xgrad[:, s * side:(s + 1) * side] = xacc[s].astype(BF)


def layer(pattern, slot, x, c, store):
    n_rows, width = x.shape
    slots, side, _ = store.shape
    tiles = pattern.shape[1]
    row_blocks = width // side
    smem = pl.BlockSpec(memory_space=pltpu.SMEM)
    vmem = pl.BlockSpec(memory_space=pltpu.VMEM)
    return pl.pallas_call(
        layer_kernel,
        out_shape=(
            jax.ShapeDtypeStruct(x.shape, BF),
            jax.ShapeDtypeStruct(x.shape, BF),
            jax.ShapeDtypeStruct((row_blocks + tiles + 1, n_rows, side), BF),
            jax.ShapeDtypeStruct((2 * tiles + row_blocks, n_rows, side), BF),
            jax.ShapeDtypeStruct((slots,), jnp.int32),
            jax.ShapeDtypeStruct((slots,), jnp.int32),
        ),
        in_specs=[smem, smem, vmem, vmem, pl.BlockSpec(memory_space=pl.ANY)],
        out_specs=(vmem, vmem, vmem, vmem, smem, smem),
        scratch_shapes=[
            pltpu.SMEM((tiles,), jnp.int32),
            pltpu.SMEM((FF // side,), jnp.int32),
            pltpu.VMEM((2, tiles, side, side), BF),
            pltpu.VMEM((tiles, side, side), BF),
            pltpu.VMEM((tiles, n_rows, 2 * side), F32),
            pltpu.VMEM((tiles, n_rows, side), F32),
            pltpu.VMEM((row_blocks, n_rows, side), F32),
            pltpu.VMEM((row_blocks, n_rows, side), F32),
            pltpu.SemaphoreType.DMA((2,)),
        ],
        compiler_params=pltpu.CompilerParams(vmem_limit_bytes=VMEM_BYTES),
    )(pattern, slot, x, c, store)


def place():
    me = lax.axis_index("fsdp")
    return me // 4, lax.rem(me // 2, 2), lax.rem(me, 2)


def at(z, y, c):
    return (z * 2 + y) * 2 + c


def greet(partners):
    barrier = pltpu.get_barrier_semaphore()
    for ok, dev in partners:
        if ok is None:
            pl.semaphore_signal(barrier, inc=1, device_id=dev, device_id_type=pl.DeviceIdType.MESH)
        else:
            @pl.when(ok)
            def _():
                pl.semaphore_signal(barrier, inc=1, device_id=dev, device_id_type=pl.DeviceIdType.MESH)
    count = sum(1 if ok is None else ok.astype(jnp.int32) for ok, _ in partners)
    pl.semaphore_wait(barrier, count)


def remote(src, dst, send_sem, recv_sem, dev):
    return pltpu.make_async_remote_copy(
        src_ref=src, dst_ref=dst, send_sem=send_sem, recv_sem=recv_sem,
        device_id=dev, device_id_type=pl.DeviceIdType.MESH,
    )


N_CHUNK = 4
N_BOTH = 2
N_HALF = 1


def gather_kernel(store, full, hold, local_sem, send_sem, recv_sem):
    z, y, c = place()
    g = lax.axis_index("groups")
    cap = store.shape[0]
    size = cap // N_CHUNK
    dev_up = {"fsdp": at(z + 1, y, c)}
    dev_down = {"fsdp": at(z - 1, y, c)}
    dev_y = {"fsdp": at(z, 1 - y, c)}
    dev_x = {"groups": 1 - g}
    dev_core = {"fsdp": at(z, y, 1 - c)}
    greet([(z < 3, dev_up), (z > 0, dev_down), (None, dev_y), (None, dev_x), (None, dev_core)])

    def rows(owner, k):
        return full.at[pl.ds(owner * cap + k * size, size)]

    def copy(way, dev, owner, k, src=None):
        dst = rows(owner, k)
        return remote(dst if src is None else src, dst, send_sem.at[way, owner // 2, k], recv_sem.at[owner, k], dev)

    def send(way, dev, owner, k, act, src=None):
        d = copy(way, dev, owner, k, src)
        d.start() if act else d.wait_send()

    def chunk(i):
        return jnp.where(i < N_HALF, N_BOTH + g * N_HALF + i, i - N_HALF)

    def other(i):
        return N_BOTH + (1 - g) * N_HALF + i

    own = at(z, y, c)
    load = pltpu.make_async_copy(store, hold, local_sem.at[0])
    keep = pltpu.make_async_copy(hold, full.at[pl.ds(own * cap, cap)], local_sem.at[1])

    def own_sends(act):
        def body(i, carry):
            k = chunk(i)
            src = store.at[pl.ds(k * size, size)]

            @pl.when(z < 3)
            def _():
                send(0, dev_up, own, k, act, src)

            @pl.when(z > 0)
            def _():
                send(1, dev_down, own, k, act, src)

            send(2, dev_y, own, k, act, src)
            return carry

        lax.fori_loop(0, N_BOTH + N_HALF, body, 0)

        def body_core(k, carry):
            send(4, dev_core, own, k, act, store.at[pl.ds(k * size, size)])
            return carry

        lax.fori_loop(0, N_CHUNK, body_core, 0)

    def line(d, act):
        def body(i, carry):
            k = chunk(i)
            for below in (True, False):
                src_z = z - d if below else z + d
                owner = at(src_z, y, c)

                @pl.when((src_z >= 0) if below else (src_z <= 3))
                def _():
                    if act:
                        copy(0, dev_core, owner, k).wait_recv()

                    @pl.when((z < 3) if below else (z > 0))
                    def _():
                        if below:
                            send(0, dev_up, owner, k, act)
                        else:
                            send(1, dev_down, owner, k, act)

                    send(2, dev_y, owner, k, act)

                    @pl.when(i < N_HALF)
                    def _():
                        send(3, dev_x, owner, k, act)

                    send(4, dev_core, owner, k, act)

            return carry

        lax.fori_loop(0, N_BOTH + N_HALF, body, 0)

    def across_y(d, act):
        def body(i, carry):
            k = chunk(i)
            for src_z in ((z,) if d == 0 else (z - d, z + d)):
                owner = at(src_z, 1 - y, c)

                @pl.when((src_z >= 0) & (src_z <= 3))
                def _():
                    if act:
                        copy(0, dev_core, owner, k).wait_recv()

                    @pl.when(i < N_HALF)
                    def _():
                        send(3, dev_x, owner, k, act)

                    send(4, dev_core, owner, k, act)

            return carry

        lax.fori_loop(0, N_BOTH + N_HALF, body, 0)

    def across_x(d, act):
        def body(i, carry):
            k = other(i)
            for src_z in ((z,) if d == 0 else (z - d, z + d)):
                for yy in ((1 - y,) if d == 0 else (y, 1 - y)):
                    owner = at(src_z, yy, c)

                    @pl.when((src_z >= 0) & (src_z <= 3))
                    def _():
                        if act:
                            copy(0, dev_core, owner, k).wait_recv()
                        send(4, dev_core, owner, k, act)

            return carry

        lax.fori_loop(0, N_HALF, body, 0)

    own_sends(True)
    load.start()
    load.wait()
    keep.start()
    steps = ((line, 1), (across_y, 0), (line, 2), (across_y, 1), (across_x, 0), (line, 3), (across_x, 1),
             (across_y, 2), (across_x, 2), (across_y, 3), (across_x, 3))
    for step, d in steps:
        step(d, True)

    def core_in(i, carry):
        owner = (i // N_CHUNK) * 2 + 1 - c
        copy(0, dev_core, owner, lax.rem(i, N_CHUNK)).wait_recv()
        return carry

    lax.fori_loop(0, 8 * N_CHUNK, core_in, 0)
    keep.wait()
    own_sends(False)
    for step, d in steps:
        step(d, False)


def gather_tiles(store):
    cap, side, _ = store.shape
    return pl.pallas_call(
        gather_kernel,
        out_shape=jax.ShapeDtypeStruct((16 * cap, side, side), BF),
        in_specs=[pl.BlockSpec(memory_space=pl.ANY)],
        out_specs=pl.BlockSpec(memory_space=pl.ANY),
        scratch_shapes=[
            pltpu.VMEM(store.shape, BF),
            pltpu.SemaphoreType.DMA((2,)),
            pltpu.SemaphoreType.DMA((5, 8, N_CHUNK)),
            pltpu.SemaphoreType.DMA((16, N_CHUNK)),
        ],
        compiler_params=pltpu.CompilerParams(collective_id=0, has_side_effects=True),
    )(store)


def scatter_kernel(
    lidx, ridx, left, right, out, part, core_in, y_in, lo_in, hi_in, far_lo, far_hi, far_y,
    core_s, core_r, y_s, y_r, z_s, lo_r, hi_r, far_s, far_lo_r, far_hi_r, far_y_sem,
):
    z, y, c = place()
    cap = out.shape[0]
    few = far_y.shape[0]
    dev_up = {"fsdp": at(z + 1, y, c)}
    dev_down = {"fsdp": at(z - 1, y, c)}
    dev_y = {"fsdp": at(z, 1 - y, c)}
    dev_core = {"fsdp": at(z, y, 1 - c)}
    greet([(z < 3, dev_up), (z > 0, dev_down), (None, dev_y), (None, dev_core)])

    def order(t):
        base = jnp.where((z == 0) | (z == 3), 3 - t, (3, 0, 2, 1)[t])
        return jnp.where(z >= 2, 3 - base, base)

    def compute(owner):
        def body(i, carry):
            s = owner * cap + i
            part[s] = dot(left[lidx[s]], right[ridx[s]], 0, 0).astype(BF)
            return carry

        lax.fori_loop(0, cap, body, 0, unroll=4)

    def mine(owner):
        return part.at[pl.ds(owner * cap, cap)]

    def core_copy(o, yy):
        return remote(mine(at(o, yy, 1 - c)), core_in.at[o * 2 + yy], core_s.at[o * 2 + yy], core_r.at[o * 2 + yy], dev_core)

    def y_copy(o):
        rest = pl.ds(at(o, 1 - y, c) * cap + few, cap - few)
        return remote(part.at[rest], y_in.at[o, pl.ds(few, cap - few)], y_s.at[o], y_r.at[o], dev_y)

    def up_copy(o):
        return remote(mine(at(o, y, c)), lo_in.at[o], z_s.at[o], lo_r.at[o], dev_up)

    def down_copy(o):
        return remote(mine(at(o, y, c)), hi_in.at[o], z_s.at[o], hi_r.at[o], dev_down)

    def far_rows(o):
        return part.at[pl.ds(at(o, 1 - y, c) * cap, few)]

    def far_up(o):
        return remote(far_rows(o), far_lo.at[o], far_s.at[o], far_lo_r.at[o], dev_up)

    def far_down(o):
        return remote(far_rows(o), far_hi.at[o], far_s.at[o], far_hi_r.at[o], dev_down)

    def far_y_copy():
        return remote(far_rows(z), far_y, far_y_sem.at[0], far_y_sem.at[1], dev_y)

    def add(owner, terms, start, stop, final=False):
        def body(i, carry):
            s = owner * cap + i
            total = part[s].astype(F32)
            for get in terms:
                total += get(i).astype(F32)
            if final:
                out[i] = total
            else:
                part[s] = total.astype(BF)
            return carry

        lax.fori_loop(start, stop, body, 0, unroll=2)

    def chain(t, o, up, down, lo, hi, total):
        if t < 3:
            @pl.when(o < z)
            def _():
                @pl.when(z < 3)
                def _():
                    down(o).wait_recv()
                    total([lambda i: hi[o, i]])

                @pl.when(z == 3)
                def _():
                    total([])

                down(o).start()

            @pl.when(o > z)
            def _():
                @pl.when(z > 0)
                def _():
                    up(o).wait_recv()
                    total([lambda i: lo[o, i]])

                @pl.when(z == 0)
                def _():
                    total([])

                up(o).start()
        else:
            @pl.when(z < 3)
            def _():
                down(o).wait_recv()

            @pl.when(z > 0)
            def _():
                up(o).wait_recv()

            @pl.when(z == 0)
            def _():
                total([lambda i: hi[o, i]])

            @pl.when(z == 3)
            def _():
                total([lambda i: lo[o, i]])

            @pl.when((z > 0) & (z < 3))
            def _():
                total([lambda i: hi[o, i], lambda i: lo[o, i]])

    def to_core(o):
        compute(at(o, 1 - y, 1 - c))
        core_copy(o, 1 - y).start()

    def to_y(o):
        compute(at(o, 1 - y, c))
        core_copy(o, 1 - y).wait_recv()
        add(at(o, 1 - y, c), [lambda i: core_in[o * 2 + 1 - y, i]], few, cap)
        y_copy(o).start()

    def far_step(t, o):
        def total(terms):
            add(at(o, 1 - y, c), [lambda i: core_in[o * 2 + 1 - y, i]] + terms, 0, few)

        chain(t, o, far_up, far_down, far_lo, far_hi, total)

    to_core(order(0))
    for t in range(4):
        if t < 3:
            to_core(order(t + 1))
        to_y(order(t))
        if t > 0:
            far_step(t - 1, order(t - 1))
    for t in range(4):
        o = order(t)
        compute(at(o, y, 1 - c))
        core_copy(o, y).start()
    far_step(3, order(3))
    far_y_copy().start()
    for t in range(4):
        compute(at(order(t), y, c))
    def near_step(t, o):
        final = t == 3
        core_copy(o, y).wait_recv()
        y_copy(o).wait_recv()
        if final:
            far_y_copy().wait_recv()

        def total(terms):
            terms = [lambda i: core_in[o * 2 + y, i]] + terms
            add(at(o, y, c), terms + ([lambda i: far_y[i]] if final else []), 0, few, final)
            add(at(o, y, c), terms + [lambda i: y_in[o, i]], few, cap, final)

        chain(t, o, up_copy, down_copy, lo_in, hi_in, total)

    for t in range(4):
        near_step(t, order(t))
    for t in range(4):
        o = order(t)
        core_copy(o, y).wait_send()
        core_copy(o, 1 - y).wait_send()
        y_copy(o).wait_send()
        if t < 3:
            up_copy(o).wait_send()
            far_up(o).wait_send()
    far_y_copy().wait_send()


def scatter_grads(lidx, ridx, left, right):
    slots = lidx.shape[0]
    cap = slots // 16
    few = 3 * cap // 16
    side = left.shape[2]
    vmem = pl.BlockSpec(memory_space=pltpu.VMEM)
    smem = pl.BlockSpec(memory_space=pltpu.SMEM)
    dma = pltpu.SemaphoreType.DMA
    return pl.pallas_call(
        scatter_kernel,
        out_shape=jax.ShapeDtypeStruct((cap, side, side), F32),
        in_specs=[smem, smem, vmem, vmem],
        out_specs=vmem,
        scratch_shapes=[
            pltpu.VMEM((slots, side, side), BF),
            pltpu.VMEM((8, cap, side, side), BF),
            pltpu.VMEM((4, cap, side, side), BF),
            pltpu.VMEM((4, cap, side, side), BF),
            pltpu.VMEM((4, cap, side, side), BF),
            pltpu.VMEM((4, few, side, side), BF),
            pltpu.VMEM((4, few, side, side), BF),
            pltpu.VMEM((few, side, side), BF),
            dma((8,)), dma((8,)), dma((4,)), dma((4,)), dma((4,)), dma((4,)), dma((4,)),
            dma((4,)), dma((4,)), dma((4,)), dma((2,)),
        ],
        compiler_params=pltpu.CompilerParams(
            collective_id=1, has_side_effects=True, vmem_limit_bytes=VMEM_BYTES
        ),
    )(lidx, ridx, left, right)


def grads_kernel(lidx, ridx, left, right, grads):
    def body(s, carry):
        grads[s] = dot(left[lidx[s]], right[ridx[s]], 0, 0).astype(BF)
        return carry

    lax.fori_loop(0, grads.shape[0], body, 0, unroll=4)


def local_grads(lidx, ridx, left, right):
    vmem = pl.BlockSpec(memory_space=pltpu.VMEM)
    smem = pl.BlockSpec(memory_space=pltpu.SMEM)
    side = left.shape[2]
    return pl.pallas_call(
        grads_kernel,
        out_shape=jax.ShapeDtypeStruct((lidx.shape[0], side, side), BF),
        in_specs=[smem, smem, vmem, vmem],
        out_specs=vmem,
        compiler_params=pltpu.CompilerParams(vmem_limit_bytes=VMEM_BYTES),
    )(lidx, ridx, left, right)


def on_device(on_grid, inputs, cotangent, tile_store, pattern, tile_slot):
    if on_grid:
        gathered = gather_tiles(tile_store)
    else:
        gathered = lax.all_gather(tile_store, "fsdp", axis=0, tiled=True)
    output, input_grad, left, right, lidx, ridx = layer(pattern, tile_slot, inputs, cotangent, gathered)
    if on_grid:
        tile_grads = scatter_grads(lidx, ridx, left, right)
    else:
        grads = local_grads(lidx, ridx, left, right)
        tile_grads = lax.psum_scatter(grads, "fsdp", scatter_dimension=0, tiled=True).astype(F32)
    return output, input_grad, tile_grads


def solution(mesh):
    placed = (
        P(("groups", "fsdp"), None),
        P(("groups", "fsdp"), None),
        P("fsdp", None, None),
        P(),
        P(),
    )
    on_grid = mesh.shape["fsdp"] == 16 and mesh.shape["groups"] == 2
    return jax.shard_map(
        functools.partial(on_device, on_grid),
        mesh=mesh,
        in_specs=placed,
        out_specs=(
            P(("groups", "fsdp"), None),
            P(("groups", "fsdp"), None),
            P(("groups", "fsdp"), None, None),
        ),
        check_vma=False,
    )
```
